256 devices in a mesh: grp: 32 (over z, y), tp: 8 (over x, core).
Axes of the slice: x: 4, y: 4, z: 8, core: 2. Of those that a mesh axis runs over, the one named last changes fastest.
Arguments:
- hidden: bfloat16 [8192, 7168], P('grp', 'tp'), may hold values from -6 to 6
- w_dkv: bfloat16 [7168, 576], P('tp'), may hold values from -0.0625 to 0.0625
- kv_gain: float32 [512], replicated, may hold values from 0.1 to 1.9
- queries: bfloat16 [8192, 24576], P('grp', 'tp'), may hold values from -18 to 18
- w_uk: bfloat16 [512, 16384], P(None, 'tp'), may hold values from -0.5 to 0.5
- w_uv: bfloat16 [512, 16384], P(None, 'tp'), may hold values from -0.25 to 0.25
- store: bfloat16 [1024, 576, 128], P('grp'), may hold values from -18 to 18
- page_table: int32 [128, 8], replicated, may hold values from 0 to 1023, as said below
- cached_len: int32 [128], replicated, may hold values from 512 to 1024
- app_len: int32 [128], replicated, may hold values from 16 to 64
Outputs:
- attended: bfloat16 [8192, 16384], P('grp', 'tp')
The draws below stay inside these ranges and needn't reach their ends.
Inputs may be any that keep to these rules, and one draw needn't show every extreme that they name: `page_table`: every store page is named once. The pages of the trajectories resumed on decode group g (rows g * 4 to (g + 1) * 4 - 1) lie exactly 1 in each block of 32 store pages.
All inputs are finite; a program needn't handle non-finite values.
Results may differ from the reference program's by a relative error of at most 0.0072.
Values may be sent and summed in bfloat16 or wider, within the bound.
A program may use at most 128 MiB of HBM per device.

```python
import math
import jax
import jax.numpy as jnp
from jax import lax

D = 7168
HEADS = 128
NOPE = 128
ROPE = 64
LAT = 512
VHEAD = 128
PAGE = 128
MAXP = 8
TR_G = 4
APP = 64
KVW = 576
TRAJS = 128
TOKENS = 8192
P_G = 32


def draw_queries(key, part):
    key = jax.random.fold_in(key, 11)
    first = jax.random.fold_in(key, 0)
    shape = (TOKENS, HEADS, NOPE + ROPE)
    values = jnp.clip(jax.random.normal(first, shape, jnp.float32), -6.0, 6.0)
    return values.reshape(TOKENS, HEADS * (NOPE + ROPE)).astype(jnp.bfloat16)


def draw_store(key, part):
    key = jax.random.fold_in(key, 7)
    first = jax.random.fold_in(key, 0)
    shape = (TRAJS * MAXP, KVW, PAGE)
    values = jnp.clip(jax.random.normal(first, shape, jnp.float32), -6.0, 6.0)
    return values.astype(jnp.bfloat16)


def draw_page_table(key, part):
    key = jax.random.fold_in(key, 5)
    first, second = jax.random.split(key, 2)
    groups = TRAJS // TR_G
    share = P_G // groups
    shuffled = jax.vmap(lambda k: jax.random.permutation(k, P_G))(jax.random.split(first, groups))
    blocks = shuffled.reshape(groups, groups, share) + (jnp.arange(groups) * P_G)[:, None, None]
    per_target = jnp.transpose(blocks, (1, 0, 2)).reshape(groups, P_G)
    mixing = jax.vmap(lambda k: jax.random.permutation(k, P_G))(jax.random.split(second, groups))
    per_target = jnp.take_along_axis(per_target, mixing, axis=1)
    return per_target.reshape(TRAJS, MAXP).astype(jnp.int32)


def set_ends(entries, own_key, low, largest):
    spot = [jax.random.randint(jax.random.fold_in(own_key, axis), (), 0, length) for axis, length in enumerate(entries.shape)]
    longest = entries.shape.index(max(entries.shape))
    next_to = spot[:longest] + [(spot[longest] + 1) % entries.shape[longest]] + spot[longest + 1:]
    return entries.at[tuple(spot)].set(low).at[tuple(next_to)].set(largest)


def block_scale(own_key, extent, shards, smallest, top_value):
    level = 1.0
    for axis_at, blocks in shards:
        draws = jax.random.uniform(jax.random.fold_in(jax.random.fold_in(own_key, 6), axis_at), (blocks,), jnp.float32, smallest / len(shards), top_value / len(shards))
        level = level * jnp.repeat(jnp.exp(draws), extent[axis_at] // blocks).reshape((-1,) + (1,) * (len(extent) - 1 - axis_at))
    return level


def noise(stream_key, extent, spread, bound, cuts=(), kind=jnp.bfloat16):
    loudness = block_scale(stream_key, extent, cuts, -0.22, 0.18) if cuts else 1.0
    drawn = jax.random.normal(stream_key, extent, jnp.float32) * spread * loudness
    return jnp.minimum(jnp.maximum(drawn, -bound), bound).astype(kind)


def setup_inputs(seed: int = 0) -> dict:
    seeds = jax.random.split(jax.random.key(seed), 11)
    return {
        "hidden": noise(seeds[0], (TOKENS, D), 1.0, 6.0, ((0, 32), (1, 8))),
        "w_dkv": noise(seeds[1], (D, KVW), D ** -0.5, 0.0625, ((0, 8),)),
        "kv_gain": jnp.clip(1.0 + 0.18 * jax.random.normal(seeds[2], (LAT,), jnp.float32), 0.1, 1.9),
        "queries": draw_queries(jax.random.fold_in(seeds[10], 71), 0),
        "w_uk": noise(seeds[4], (LAT, HEADS * NOPE), NOPE ** -0.5, 0.5, ((1, 8),)),
        "w_uv": noise(seeds[5], (LAT, HEADS * VHEAD), LAT ** -0.5, 0.25, ((1, 8),)),
        "store": draw_store(jax.random.fold_in(seeds[10], 71), 0),
        "page_table": draw_page_table(jax.random.fold_in(seeds[10], 71), 0),
        "cached_len": set_ends(jax.random.randint(seeds[8], (TRAJS,), MAXP * PAGE // 2, MAXP * PAGE + 1), jax.random.fold_in(seeds[8], 1), MAXP * PAGE // 2, MAXP * PAGE).astype(jnp.int32),
        "app_len": set_ends(jax.random.randint(seeds[9], (TRAJS,), max(1, APP // 4), APP + 1), jax.random.fold_in(seeds[9], 1), max(1, APP // 4), APP).astype(jnp.int32),
    }


def angle_table(positions, width):
    half = width // 2
    freq = jnp.exp(jnp.arange(half).astype(jnp.float32) * (-2.0 * math.log(10000.0) / width))
    return positions.astype(jnp.float32)[:, None] * freq[None, :]

def rotate(vec, angles):
    half = vec.shape[-1] // 2
    first = vec[..., :half]
    second = vec[..., half:]
    cosine = jnp.cos(angles)
    sine = jnp.sin(angles)
    return jnp.concatenate([first * cosine - second * sine, first * sine + second * cosine], axis=-1)

def finish_keys(kv, positions, kv_gain, lat_width):
    latent = kv[:, :lat_width]
    factor = lax.rsqrt(lax.optimization_barrier(jnp.mean(latent * latent, axis=-1, keepdims=True)) + 1e-06)
    latent = latent * factor * kv_gain.astype(jnp.float32)[None, :]
    rotary = rotate(kv[:, lat_width:], angle_table(positions, kv.shape[1] - lat_width))
    return jnp.concatenate([latent, rotary], axis=-1).astype(jnp.bfloat16)

def attend_ref(q_full, pages, fresh, length, count, w_uv3):
    rows = q_full.shape[0]
    factor = 1.0 / math.sqrt(NOPE + ROPE)
    qf = q_full.astype(jnp.float32)
    cache = jnp.transpose(pages, (1, 0, 2)).reshape(KVW, MAXP * PAGE).astype(jnp.float32)
    keys = jnp.concatenate([cache.T, fresh.astype(jnp.float32)], axis=0)
    scores = jnp.einsum('qhc,kc->hqk', qf, keys) * factor
    spots = jnp.arange(MAXP * PAGE, dtype=jnp.int32)
    slots = jnp.arange(rows, dtype=jnp.int32)
    old_ok = jnp.broadcast_to((spots < length)[None, :], (rows, MAXP * PAGE))
    new_ok = (slots[None, :] <= slots[:, None]) & (slots[None, :] < count)
    allowed = jnp.concatenate([old_ok, new_ok], axis=1)
    scores = jnp.where(allowed[None], scores, -jnp.inf)
    top = lax.optimization_barrier(jnp.max(scores, axis=-1, keepdims=True))
    expo = jnp.exp(scores - top)
    probs = (expo / lax.optimization_barrier(jnp.sum(expo, axis=-1, keepdims=True))).astype(jnp.bfloat16)
    o_lat = jnp.einsum('hqk,kc->qhc', probs.astype(jnp.float32), keys[:, :LAT]).astype(jnp.bfloat16)
    out = jnp.einsum('qhc,chv->qhv', o_lat.astype(jnp.float32), w_uv3)
    out = jnp.where((slots < count)[:, None, None], out, 0.0)
    return out.reshape(rows, -1).astype(jnp.bfloat16)

def reference(hidden, w_dkv, kv_gain, queries, w_uk, w_uv, store, page_table, cached_len, app_len):
    width = NOPE + ROPE
    w_uk3 = w_uk.astype(jnp.float32).reshape(LAT, HEADS, NOPE)
    w_uv3 = w_uv.astype(jnp.float32).reshape(LAT, HEADS, VHEAD)

    def one(traj):
        start = (traj * APP).astype(jnp.int32)
        rows = lax.dynamic_slice_in_dim(hidden, start, APP, 0)
        kv = jnp.dot(rows, w_dkv, preferred_element_type=jnp.float32)
        positions = cached_len[traj] + jnp.arange(APP, dtype=jnp.int32)
        fresh = finish_keys(kv, positions, kv_gain, LAT)
        q = lax.dynamic_slice_in_dim(queries, start, APP, 0).reshape(APP, HEADS, width)
        q_lat = jnp.einsum('qhn,lhn->qhl', q[..., :NOPE].astype(jnp.float32), w_uk3).astype(jnp.bfloat16)
        q_rope = rotate(q[..., NOPE:].astype(jnp.float32), angle_table(positions, ROPE)[:, None, :]).astype(jnp.bfloat16)
        q_full = jnp.concatenate([q_lat, q_rope], axis=-1)
        pages = store[page_table[traj]]
        return attend_ref(q_full, pages, fresh, cached_len[traj], app_len[traj], w_uv3)
    outs = lax.map(one, jnp.arange(TRAJS, dtype=jnp.int32))
    return outs.reshape(TRAJS * APP, HEADS * VHEAD)
```

```python
import functools
import math

import jax
import jax.numpy as jnp
from jax import lax
from jax.experimental import pallas as pl
from jax.experimental.pallas import tpu as pltpu
from jax.sharding import PartitionSpec as P

MESH = pl.DeviceIdType.MESH
NOPE = 128
ROPE = 64
LAT = 512
VHEAD = 128
PAGE = 128
MAXP = 8
TR_G = 4
APP = 64
KVW = LAT + ROPE
HALF = KVW // 2
NEG = -1e30
NT = (((1,), (1,)), ((), ()))


def rem(a, n):
    return lax.rem(a + n, n)


def hop_order(Z):
    odd = sorted(range(1, Z, 2), key=lambda d: (min(d, Z - d), d))
    even = sorted(range(2, Z, 2), key=lambda d: (min(d, Z - d), d))
    return odd, even


def tables(pos, width):
    half = width // 2
    lane = lax.rem(lax.broadcasted_iota(jnp.int32, (1, width), 1), half)
    freq = jnp.exp(lane.astype(jnp.float32) * (-2.0 * math.log(10000.0) / width))
    angle = pos.astype(jnp.float32) * freq
    sign = jnp.where(lax.broadcasted_iota(jnp.int32, (1, width), 1) < half, -1.0, 1.0)
    return jnp.cos(angle), jnp.sin(angle) * sign


def rotate(vec, cosine, sine):
    half = vec.shape[1] // 2
    swapped = jnp.concatenate([vec[:, half:], vec[:, :half]], axis=1)
    return vec * cosine + swapped * sine


def move_kernel(
    Z, Y, X,
    pt_ref, len_ref, gain_ref, hidden_hbm, wdkv_hbm, queries_hbm, wuk_hbm, store_hbm,
    pages_hbm, q_hbm, fresh_hbm,
    store_v, staging, pages, hidden, wdkv, queries, wuk, q_v, kv_part, kv_half, kv_sib, kv_in, fresh,
    load_sem, out_sem, bar_unused, send1, recv, recv2, sendx, sendr, sends, kvsend, kvrecv,
):
    G = Z * Y
    g = lax.axis_index("grp")
    tp = lax.axis_index("tp")
    z, y = g // Y, lax.rem(g, Y)
    x, c = tp // 2, lax.rem(tp, 2)
    odd, even = hop_order(Z)
    KS = len(odd)
    KE = len(even)

    loads = [
        pltpu.make_async_copy(store_hbm, store_v, load_sem.at[0]),
        pltpu.make_async_copy(hidden_hbm, hidden, load_sem.at[1]),
        pltpu.make_async_copy(wdkv_hbm, wdkv, load_sem.at[2]),
        pltpu.make_async_copy(queries_hbm, queries, load_sem.at[3]),
        pltpu.make_async_copy(wuk_hbm, wuk, load_sem.at[4]),
    ]
    for load in loads:
        load.start()

    xr, xl, xo = rem(x + 1, X), rem(x - 1, X), rem(x + 2, X)
    dev_r, dev_l, dev_o, dev_s = (
        (g, xr * 2 + c), (g, xl * 2 + c), (g, xo * 2 + c), (g, x * 2 + 1 - c)
    )

    def hop(k):
        return jnp.where(c == 1, odd[k], even[k] if k < KE else odd[k])

    def to_group(dz, dy):
        return rem(z + dz, Z) * Y + rem(y + dy, Y)

    def dy_of(dz):
        return lax.rem(dz + x, Y)

    def both(k, fn):
        if k < KE:
            fn()
        else:
            pl.when(c == 1)(fn)

    def direct(d, fn):
        pl.when(c == (1 if d == Y - 1 else 0))(fn)

    barrier = pltpu.get_barrier_semaphore()

    def greet(dev):
        pl.semaphore_signal(barrier, inc=1, device_id=dev, device_id_type=MESH)

    for dev in (dev_r, dev_l, dev_o, dev_s):
        greet(dev)
    for k in range(KS):
        both(k, lambda: greet((to_group(-hop(k), -dy_of(hop(k))), tp)))
    for d in range(1, Y):
        direct(d, lambda: greet((to_group(0, -d), tp)))

    def find(dest):
        found = jnp.int32(0)
        for t in range(TR_G):
            for m in range(MAXP):
                value = pt_ref[dest * TR_G + t, m]
                found = found + jnp.where(value // G == g, lax.rem(value, G), 0)
        return found

    picks = []
    for k in range(KS):
        picks.append(find(to_group(hop(k), dy_of(hop(k)))))
    mine = find(g)
    d_one = jnp.where(c == 1, Y - 1, 1)
    pick_one = find(to_group(0, d_one))
    pick_two = find(to_group(0, 2))

    loads[0].wait()
    for k in range(KS):
        staging[k] = store_v[picks[k]]
    staging[KS] = store_v[pick_one]
    staging[KS + 1] = store_v[pick_two]
    pages[0] = store_v[mine]

    pl.semaphore_wait(barrier, KS + 5)

    def rcopy(src, dst, ss, rs, dev):
        return pltpu.make_async_remote_copy(
            src_ref=src, dst_ref=dst, send_sem=ss, recv_sem=rs, device_id=dev, device_id_type=MESH
        )

    def first(k):
        dz = hop(k)
        slot = dz * Y + x
        return rcopy(staging.at[k], pages.at[slot], send1.at[k], recv.at[slot], (to_group(dz, dy_of(dz)), tp))

    def first_direct(d):
        at = KS + (1 if d == 2 else 0)
        return rcopy(staging.at[at], pages.at[d], send1.at[at], recv.at[d], (to_group(0, d), tp))

    for k in range(KS):
        both(k, lambda: first(k).start())
    for d in range(1, Y):
        direct(d, lambda: first_direct(d).start())

    loads[1].wait()
    loads[2].wait()
    rows = hidden.shape[0]
    hrows = rows // 2
    brows = hrows // X
    kv_part[...] = jnp.dot(hidden[...], wdkv[...], preferred_element_type=jnp.float32)
    sib_kv = rcopy(kv_part.at[pl.ds((1 - c) * hrows, hrows)], kv_sib, kvsend.at[0], kvrecv.at[0], dev_s)
    sib_kv.start()

    tok = lax.broadcasted_iota(jnp.int32, (APP, 1), 0)
    pos = jnp.concatenate([tok + len_ref[g * TR_G + t] for t in range(TR_G)], axis=0)
    cosine, sine = tables(pos, ROPE)

    sib_kv.wait()
    kv_half[...] = kv_part[pl.ds(c * hrows, hrows), :] + kv_sib[...]
    kv_x = []
    for n, (xx, dev) in enumerate(((xr, dev_r), (xl, dev_l), (xo, dev_o))):
        copy = rcopy(kv_half.at[pl.ds(xx * brows, brows)], kv_in.at[n], kvsend.at[1 + n], kvrecv.at[1 + n], dev)
        copy.start()
        kv_x.append(copy)

    loads[3].wait()
    loads[4].wait()
    heads = wuk.shape[1] // NOPE
    blocks = rows // 16

    def q_head(h):
        base = h * (NOPE + ROPE)
        nope = queries[:, base : base + NOPE]
        lat = lax.dot_general(
            nope, wuk[:, h * NOPE : (h + 1) * NOPE], NT, preferred_element_type=jnp.float32
        ).astype(jnp.bfloat16)
        rot = rotate(queries[:, base + NOPE : base + NOPE + ROPE].astype(jnp.float32), cosine, sine)
        q_v[:, h * 16 : (h + 1) * 16, 0:LAT] = lat.reshape(blocks, 16, LAT)
        q_v[:, h * 16 : (h + 1) * 16, LAT:KVW] = rot.astype(jnp.bfloat16).reshape(blocks, 16, ROPE)

    for h in range(heads // 2):
        q_head(h)

    for copy in kv_x:
        copy.wait()
    kv = kv_half[pl.ds(x * brows, brows), :] + kv_in[0] + kv_in[1] + kv_in[2]
    lat = kv[:, :LAT]
    factor = lax.rsqrt(jnp.mean(lat * lat, axis=-1, keepdims=True) + 1e-06)
    lat = lat * factor * gain_ref[...]
    row0 = c * hrows + x * brows
    mypos = len_ref[g * TR_G + row0 // APP] + lax.rem(row0, APP)
    mycos, mysin = tables(mypos + lax.broadcasted_iota(jnp.int32, (brows, 1), 0), ROPE)
    myrope = rotate(kv[:, LAT:], mycos, mysin)
    fresh[pl.ds(row0, brows), 0:LAT] = lat.astype(jnp.bfloat16)
    fresh[pl.ds(row0, brows), LAT:KVW] = myrope.astype(jnp.bfloat16)
    fr_x = []
    for n, dev in enumerate((dev_r, dev_l, dev_o)):
        part = fresh.at[pl.ds(row0, brows)]
        copy = rcopy(part, part, kvsend.at[4 + n], kvrecv.at[4 + n], dev)
        copy.start()
        fr_x.append(copy)

    for h in range(heads // 2, heads):
        q_head(h)
    q_out = pltpu.make_async_copy(q_v, q_hbm, out_sem.at[0])
    q_out.start()

    def to_sib(slot, n):
        return rcopy(pages.at[slot], pages.at[slot], sends.at[n], recv.at[slot], dev_s)

    def to_x(slot, k, n, dev):
        return rcopy(pages.at[slot], pages.at[slot], sendx.at[k, n], recv.at[slot], dev)

    def relay(slot, k, n, dev):
        part = pages.at[slot, pl.ds(n * HALF, HALF)]
        return rcopy(part, part, sendr.at[k, n], (recv2 if n else recv).at[slot], dev)

    def slots_of(k):
        dz = hop(k) * Y
        return dz + x, dz + xl, dz + xr, dz + xo

    def own_step(k):
        own = slots_of(k)[0]
        first(k).wait_recv()
        to_x(own, k, 0, dev_r).start()
        to_x(own, k, 1, dev_l).start()
        to_sib(own, 4 * k).start()

    def side_step(k):
        _, left, right, _ = slots_of(k)
        to_x(left, k, 0, dev_r).wait_recv()
        relay(left, k, 0, dev_r).start()
        to_sib(left, 4 * k + 1).start()
        to_x(right, k, 1, dev_l).wait_recv()
        relay(right, k, 1, dev_l).start()
        to_sib(right, 4 * k + 2).start()

    def far_step(k):
        far = slots_of(k)[3]
        relay(far, k, 0, dev_r).wait_recv()
        relay(far, k, 1, dev_l).wait_recv()
        to_sib(far, 4 * k + 3).start()

    def direct_step(d):
        first_direct(d).wait_recv()
        to_sib(d, 4 * KS + (1 if d == 2 else 0)).start()

    for d in range(1, Y):
        direct(d, lambda: direct_step(d))
    for step in range(KS + 2):
        if step < KS:
            both(step, lambda: own_step(step))
        if 0 <= step - 1 < KS:
            both(step - 1, lambda: side_step(step - 1))
        if 0 <= step - 2 < KS:
            both(step - 2, lambda: far_step(step - 2))

    for copy in fr_x:
        copy.wait()
    part = fresh.at[pl.ds(c * hrows, hrows)]
    fr_s = rcopy(part, part, kvsend.at[7], kvrecv.at[7], dev_s)
    fr_s.start()

    for k in range(KS):
        other = jnp.where(c == 0, odd[k], even[k] if k < KE else odd[k]) * Y

        def take():
            for n in range(X):
                to_sib(other + n, 0).wait_recv()

        if k < KE:
            take()
        else:
            pl.when(c == 0)(take)
    for d in range(1, Y):
        pl.when(c != (1 if d == Y - 1 else 0))(lambda: to_sib(d, 0).wait_recv())
    fr_s.wait()
    f_out = pltpu.make_async_copy(fresh, fresh_hbm, out_sem.at[1])
    f_out.start()
    p_out = pltpu.make_async_copy(pages, pages_hbm, out_sem.at[2])
    p_out.start()

    def drain(k):
        first(k).wait_send()
        own, left, right, far = slots_of(k)
        to_x(own, k, 0, dev_r).wait_send()
        to_x(own, k, 1, dev_l).wait_send()
        relay(left, k, 0, dev_r).wait_send()
        relay(right, k, 1, dev_l).wait_send()
        for n, slot in enumerate((own, left, right, far)):
            to_sib(slot, 4 * k + n).wait_send()

    def drain_direct(d):
        first_direct(d).wait_send()
        to_sib(d, 4 * KS + (1 if d == 2 else 0)).wait_send()

    for k in range(KS):
        both(k, lambda: drain(k))
    for d in range(1, Y):
        direct(d, lambda: drain_direct(d))
    q_out.wait()
    f_out.wait()
    p_out.wait()


def attend_kernel(
    Z, Y,
    pt_ref, len_ref, app_ref, pages_hbm, q_hbm, fresh_hbm, wuv_hbm,
    out_ref,
    kt, q_v, fresh, wuv, s_ref, p_ref, o_ref,
    page_sem, q_sem, sem,
):
    G = Z * Y
    g = lax.axis_index("grp")
    z, y = g // Y, lax.rem(g, Y)
    f_in = pltpu.make_async_copy(fresh_hbm, fresh, sem.at[0])
    f_in.start()
    blocks = APP // 16
    q_in, page_in = [], []
    for t in range(TR_G):
        copy = pltpu.make_async_copy(
            q_hbm.at[pl.ds(t * blocks, blocks)], q_v.at[pl.ds(t * blocks, blocks)], q_sem.at[t]
        )
        copy.start()
        q_in.append(copy)
        for m in range(MAXP):
            source = pt_ref[g * TR_G + t, m] // G
            dz = rem(z - source // Y, Z)
            dy = rem(y - lax.rem(source, Y), Y)
            slot = jnp.where(dz == 0, dy, dz * Y + lax.rem(dy - dz + 2 * Z * Y, Y))
            copy = pltpu.make_async_copy(
                pages_hbm.at[slot], kt.at[t, :, pl.ds(m * PAGE, PAGE)], page_sem.at[t, m]
            )
            copy.start()
            page_in.append(copy)
    w_in = pltpu.make_async_copy(wuv_hbm, wuv, sem.at[1])
    w_in.start()
    f_in.wait()
    scale = math.log2(math.e) / math.sqrt(NOPE + ROPE)
    WIDE = 256
    heads = wuv.shape[1] // VHEAD
    for t in range(TR_G):
        q_in[t].wait()
        for m in range(MAXP):
            page_in[t * MAXP + m].wait()
        length = len_ref[g * TR_G + t]
        count = app_ref[g * TR_G + t]

        def block(jb, _):
            q = q_v[t * blocks + jb]
            top = None
            for n in range(MAXP * PAGE // WIDE):
                s = jnp.dot(q, kt[t, :, n * WIDE : (n + 1) * WIDE], preferred_element_type=jnp.float32) * scale
                if (n + 1) * WIDE > MAXP * PAGE // 2:
                    spot = n * WIDE + lax.broadcasted_iota(jnp.int32, (1, WIDE), 1)
                    s = s + jnp.where(spot < length, 0.0, NEG)
                s_ref[:, n * WIDE : (n + 1) * WIDE] = s
                part = jnp.maximum(s[:, :128], s[:, 128:])
                top = part if top is None else jnp.maximum(top, part)
            fr = fresh[t * APP : (t + 1) * APP, :]
            s = lax.dot_general(q, fr, NT, preferred_element_type=jnp.float32) * scale
            row = lax.broadcasted_iota(jnp.int32, (q.shape[0], APP), 0)
            col = lax.broadcasted_iota(jnp.int32, (q.shape[0], APP), 1)
            s = jnp.where((col <= jb * 16 + lax.rem(row, 16)) & (col < count), s, NEG)
            top = jnp.maximum(jnp.max(top, axis=1, keepdims=True), jnp.max(s, axis=1, keepdims=True))
            p = jnp.exp2(s - top)
            total = jnp.sum(p, axis=1, keepdims=True)
            acc = jnp.dot(p.astype(jnp.bfloat16), fr[:, :LAT], preferred_element_type=jnp.float32)
            sums = None
            for n in range(MAXP * PAGE // WIDE):
                p = jnp.exp2(s_ref[:, n * WIDE : (n + 1) * WIDE] - top)
                part = p[:, :128] + p[:, 128:]
                sums = part if sums is None else sums + part
                p_ref[:, n * WIDE : (n + 1) * WIDE] = p.astype(jnp.bfloat16)
            total = total + jnp.sum(sums, axis=1, keepdims=True)
            acc = acc + lax.dot_general(p_ref[...], kt[t, 0:LAT, :], NT, preferred_element_type=jnp.float32)
            o = (acc * (1.0 / total)).astype(jnp.bfloat16)
            o_ref[:, pl.ds(pl.multiple_of(t * APP + jb * 16, 16), 16), :] = o.reshape(heads, 16, LAT)
            return 0

        lax.fori_loop(0, (count + 15) // 16, block, 0)
    w_in.wait()
    tok = lax.broadcasted_iota(jnp.int32, (APP, 1), 0)
    valid = jnp.concatenate([tok < app_ref[g * TR_G + t] for t in range(TR_G)], axis=0)
    for h in range(heads):
        out = jnp.dot(o_ref[h], wuv[:, h * VHEAD : (h + 1) * VHEAD], preferred_element_type=jnp.float32)
        out_ref[:, h * VHEAD : (h + 1) * VHEAD] = jnp.where(valid, out, 0.0).astype(jnp.bfloat16)


def body(Z, Y, X, hidden, w_dkv, kv_gain, queries, w_uk, w_uv, store, page_table, cached_len, app_len):
    bf, f32 = jnp.bfloat16, jnp.float32
    rows = hidden.shape[0]
    heads = w_uk.shape[1] // NOPE
    G = Z * Y
    KS = len(hop_order(Z)[0])
    any_spec = pl.BlockSpec(memory_space=pl.ANY)
    smem = pl.BlockSpec(memory_space=pltpu.SMEM)
    vmem = pl.BlockSpec(memory_space=pltpu.VMEM)
    blocks, brow = rows // 16, heads * 16
    hrows = rows // 2
    pages, q_full, fresh = pl.pallas_call(
        functools.partial(move_kernel, Z, Y, X),
        out_shape=(
            jax.ShapeDtypeStruct((G, KVW, PAGE), bf),
            jax.ShapeDtypeStruct((blocks, brow, KVW), bf),
            jax.ShapeDtypeStruct((rows, KVW), bf),
        ),
        in_specs=[smem, smem, vmem] + [any_spec] * 5,
        out_specs=(any_spec,) * 3,
        scratch_shapes=[
            pltpu.VMEM((G, KVW, PAGE), bf),
            pltpu.VMEM((KS + 2, KVW, PAGE), bf),
            pltpu.VMEM((G, KVW, PAGE), bf),
            pltpu.VMEM(hidden.shape, bf),
            pltpu.VMEM(w_dkv.shape, bf),
            pltpu.VMEM(queries.shape, bf),
            pltpu.VMEM(w_uk.shape, bf),
            pltpu.VMEM((blocks, brow, KVW), bf),
            pltpu.VMEM((rows, KVW), f32),
            pltpu.VMEM((hrows, KVW), f32),
            pltpu.VMEM((hrows, KVW), f32),
            pltpu.VMEM((3, hrows // X, KVW), f32),
            pltpu.VMEM((rows, KVW), bf),
            pltpu.SemaphoreType.DMA((5,)),
            pltpu.SemaphoreType.DMA((3,)),
            pltpu.SemaphoreType.DMA((1,)),
            pltpu.SemaphoreType.DMA((KS + 2,)),
            pltpu.SemaphoreType.DMA((G,)),
            pltpu.SemaphoreType.DMA((G,)),
            pltpu.SemaphoreType.DMA((KS, 2)),
            pltpu.SemaphoreType.DMA((KS, 2)),
            pltpu.SemaphoreType.DMA((4 * KS + 2,)),
            pltpu.SemaphoreType.DMA((8,)),
            pltpu.SemaphoreType.DMA((8,)),
        ],
        compiler_params=pltpu.CompilerParams(
            collective_id=0, has_side_effects=True, vmem_limit_bytes=56 * 1024 * 1024
        ),
        name="move",
    )(page_table, cached_len, kv_gain[None, :], hidden, w_dkv, queries, w_uk, store)
    return pl.pallas_call(
        functools.partial(attend_kernel, Z, Y),
        out_shape=jax.ShapeDtypeStruct((rows, heads * VHEAD), bf),
        in_specs=[smem, smem, smem] + [any_spec] * 4,
        out_specs=vmem,
        scratch_shapes=[
            pltpu.VMEM((TR_G, KVW, MAXP * PAGE), bf),
            pltpu.VMEM((blocks, brow, KVW), bf),
            pltpu.VMEM((rows, KVW), bf),
            pltpu.VMEM(w_uv.shape, bf),
            pltpu.VMEM((brow, MAXP * PAGE), f32),
            pltpu.VMEM((brow, MAXP * PAGE), bf),
            pltpu.VMEM((heads, rows, LAT), bf),
            pltpu.SemaphoreType.DMA((TR_G, MAXP)),
            pltpu.SemaphoreType.DMA((TR_G,)),
            pltpu.SemaphoreType.DMA((2,)),
        ],
        compiler_params=pltpu.CompilerParams(vmem_limit_bytes=56 * 1024 * 1024),
        name="attend",
    )(page_table, cached_len, app_len, pages, q_full, fresh, w_uv)


def solution(mesh):
    X = mesh.shape["tp"] // 2
    Y = X
    Z = mesh.shape["grp"] // Y
    in_specs = (
        P("grp", "tp"),
        P("tp", None),
        P(),
        P("grp", "tp"),
        P(None, "tp"),
        P(None, "tp"),
        P("grp", None, None),
        P(),
        P(),
        P(),
    )
    return jax.shard_map(
        functools.partial(body, Z, Y, X), mesh=mesh, in_specs=in_specs, out_specs=P("grp", "tp"), check_vma=False
    )
```

```python
import functools
import math

import jax
import jax.numpy as jnp
from jax import lax
from jax.experimental import pallas as pl
from jax.experimental.pallas import tpu as pltpu
from jax.sharding import PartitionSpec as P

MESH = pl.DeviceIdType.MESH
NOPE = 128
ROPE = 64
LAT = 512
VHEAD = 128
PAGE = 128
MAXP = 8
TR_G = 4
APP = 64
KVW = LAT + ROPE
NEG = -1e30
NT = (((1,), (1,)), ((), ()))
PHASES = (32, 32, 32, 32)
CHUNK = 128
SCALE = math.log2(math.e) / math.sqrt(NOPE + ROPE)
bf16, f32 = jnp.bfloat16, jnp.float32


def rem(a, n):
    return lax.rem(a + n, n)


def tables(pos, width):
    half = width // 2
    lane = lax.rem(lax.broadcasted_iota(jnp.int32, (1, width), 1), half)
    freq = jnp.exp(lane.astype(f32) * (-2.0 * math.log(10000.0) / width))
    angle = pos.astype(f32) * freq
    sign = jnp.where(lax.broadcasted_iota(jnp.int32, (1, width), 1) < half, -1.0, 1.0)
    return jnp.cos(angle), jnp.sin(angle) * sign


def rotate(vec, cosine, sine):
    half = vec.shape[1] // 2
    swapped = jnp.concatenate([vec[:, half:], vec[:, :half]], axis=1)
    return vec * cosine + swapped * sine


def kernel(
    Z, Y, X,
    pt_ref, len_ref, app_ref, gain_ref, hidden_hbm, wdkv_hbm, queries_hbm, wuk_hbm, wuv_hbm, store_hbm,
    out_hbm,
    *scratch,
):
    n_ph = len(PHASES)
    (store_v, hidden, wdkv, queries, wuk, wuv, q_v, kv_part, kv_half, kv_sib, kv_in, fresh,
     m_ref, l_ref, acc_ref, s_a, s_b, p_ref, kt_a, kt_b, o_ref, out_v,
     load_sem, out_sem, send1, recv1, sendx, recvx, sendr, recvr, sends, recvs, kvsend, kvrecv) = scratch[: -2 * n_ph]
    stage = scratch[-2 * n_ph : -n_ph]
    pages = scratch[-n_ph:]
    s_refs, kts = (s_a, s_b), (kt_a, kt_b)
    G = Z * Y
    KC = Z // 2
    g = lax.axis_index("grp")
    tp = lax.axis_index("tp")
    z, y = g // Y, lax.rem(g, Y)
    x, c = tp // 2, lax.rem(tp, 2)
    heads = wuk.shape[1] // NOPE
    rows = hidden.shape[0]
    starts = [sum(PHASES[:i]) for i in range(n_ph)]

    loads = [
        pltpu.make_async_copy(src, dst, load_sem.at[i])
        for i, (src, dst) in enumerate(
            ((store_hbm, store_v), (hidden_hbm, hidden), (wdkv_hbm, wdkv), (queries_hbm, queries),
             (wuk_hbm, wuk), (wuv_hbm, wuv))
        )
    ]
    for load in loads:
        load.start()

    xr, xl, xo = rem(x + 1, X), rem(x - 1, X), rem(x + 2, X)
    dev_r, dev_l, dev_o, dev_s = (
        (g, xr * 2 + c), (g, xl * 2 + c), (g, xo * 2 + c), (g, x * 2 + 1 - c)
    )
    is_self = (x == 0) & (c == 0)

    def remote(k, fn):
        if k == 0:
            pl.when(jnp.logical_not(is_self))(fn)
        else:
            fn()

    def group(k, way):
        dz = 2 * k + c
        dy = lax.rem(dz + x, Y)
        return rem(z + way * dz, Z) * Y + rem(y + way * dy, Y)

    barrier = pltpu.get_barrier_semaphore()

    def greet(dev):
        pl.semaphore_signal(barrier, inc=1, device_id=dev, device_id_type=MESH)

    for dev in (dev_r, dev_l, dev_o, dev_s):
        greet(dev)
    for k in range(KC):
        remote(k, lambda: greet((group(k, -1), tp)))

    def find(dest):
        found = jnp.int32(0)
        for t in range(TR_G):
            for m in range(MAXP):
                value = pt_ref[m, dest * TR_G + t]
                found = found + jnp.where(value // G == g, lax.rem(value, G), 0)
        return found

    picks = [find(group(k, 1)) for k in range(KC)]

    def rcopy(src, dst, ss, rs, dev):
        return pltpu.make_async_remote_copy(
            src_ref=src, dst_ref=dst, send_sem=ss, recv_sem=rs, device_id=dev, device_id_type=MESH
        )

    def slot(who):
        return c * (X * KC) + who * KC

    def first(q, k):
        return rcopy(stage[q].at[k], pages[q].at[slot(x) + k], send1.at[q, k], recv1.at[q, k], (group(k, 1), tp))

    loads[0].wait()
    for k in range(KC):
        page = store_v[picks[k]]
        lat, rope = page[0:LAT, :].T, page[LAT:KVW, :].T
        for q in range(n_ph):
            stage[q][k, :, 0:LAT] = lat[starts[q] : starts[q] + PHASES[q], :]
            stage[q][k, :, LAT:KVW] = rope[starts[q] : starts[q] + PHASES[q], :]

    @pl.when(is_self)
    def _():
        for q in range(n_ph):
            pages[q][0] = stage[q][0]

    pl.semaphore_wait(barrier, KC + 4 - is_self.astype(jnp.int32))
    for q in range(n_ph):
        for k in reversed(range(KC)):
            remote(k, lambda: first(q, k).start())

    def to_x(q, who, n, dev):
        part = pages[q].at[pl.ds(slot(who), KC)]
        return rcopy(part, part, sendx.at[q, n], recvx.at[q, n], dev)

    def relay(q, who, n, dev):
        part = pages[q].at[pl.ds(slot(who) + n * (KC // 2), KC // 2)]
        return rcopy(part, part, sendr.at[q, n], recvr.at[q, n], dev)

    def to_sib(q, n):
        part = pages[q].at[pl.ds(slot((x, xl, xr, xo)[n]), KC)]
        return rcopy(part, part, sends.at[q, n], recvs.at[q, n], dev_s)

    def from_sib(q, n):
        part = pages[q].at[pl.ds((1 - c) * (X * KC) + (x, xl, xr, xo)[n] * KC, KC)]
        return rcopy(part, part, sends.at[q, n], recvs.at[q, n], dev_s)

    def step_own(q):
        for k in range(KC):
            remote(k, lambda: first(q, k).wait_recv())
        to_x(q, x, 0, dev_r).start()
        to_x(q, x, 1, dev_l).start()
        to_sib(q, 0).start()

    def step_side(q):
        to_x(q, xl, 0, dev_r).wait_recv()
        relay(q, xl, 0, dev_r).start()
        to_sib(q, 1).start()
        to_x(q, xr, 1, dev_l).wait_recv()
        relay(q, xr, 1, dev_l).start()
        to_sib(q, 2).start()

    def step_far(q):
        relay(q, xo, 0, dev_r).wait_recv()
        relay(q, xo, 1, dev_l).wait_recv()
        to_sib(q, 3).start()

    def step_done(q):
        for n in range(4):
            from_sib(q, n).wait_recv()

    hrows = rows // 2
    brows = hrows // X
    row0 = c * hrows + x * brows

    sib_kv = rcopy(kv_part.at[pl.ds((1 - c) * hrows, hrows)], kv_sib, kvsend.at[0], kvrecv.at[0], dev_s)
    kv_x = [
        rcopy(kv_half.at[pl.ds(xx * brows, brows)], kv_in.at[n], kvsend.at[1 + n], kvrecv.at[1 + n], dev)
        for n, (xx, dev) in enumerate(((xr, dev_r), (xl, dev_l), (xo, dev_o)))
    ]
    block = fresh.at[pl.ds(row0, brows)]
    fr_x = [
        rcopy(block, block, kvsend.at[4 + n], kvrecv.at[4 + n], dev)
        for n, dev in enumerate((dev_r, dev_l, dev_o))
    ]
    half = fresh.at[pl.ds(c * hrows, hrows)]
    fr_s = rcopy(half, half, kvsend.at[7], kvrecv.at[7], dev_s)

    def kv_one():
        loads[1].wait()
        loads[2].wait()
        kv_part[...] = lax.dot_general(hidden[...], wdkv[...], NT, preferred_element_type=f32)
        sib_kv.start()

    def kv_two():
        sib_kv.wait()
        kv_half[...] = kv_part[pl.ds(c * hrows, hrows), :] + kv_sib[...]
        for copy in kv_x:
            copy.start()

    def kv_three():
        for copy in kv_x:
            copy.wait()
        kv = kv_half[pl.ds(x * brows, brows), :] + kv_in[0] + kv_in[1] + kv_in[2]
        lat = kv[:, :LAT]
        factor = lax.rsqrt(jnp.mean(lat * lat, axis=-1, keepdims=True) + 1e-06)
        lat = lat * factor * gain_ref[...]
        mypos = len_ref[g * TR_G + row0 // APP] + lax.rem(row0, APP)
        mycos, mysin = tables(mypos + lax.broadcasted_iota(jnp.int32, (brows, 1), 0), ROPE)
        fresh[pl.ds(row0, brows), 0:LAT] = lat.astype(bf16)
        fresh[pl.ds(row0, brows), LAT:KVW] = rotate(kv[:, LAT:], mycos, mysin).astype(bf16)
        for copy in fr_x:
            copy.start()

    def kv_four():
        for copy in fr_x:
            copy.wait()
        fr_s.start()

    def q_heads(first_head, last_head, angles):
        cosine, sine = angles
        for h in range(first_head, last_head):
            base = h * (NOPE + ROPE)
            lat = lax.dot_general(
                queries[:, base : base + NOPE], wuk[:, h * NOPE : (h + 1) * NOPE], NT, preferred_element_type=f32
            ).astype(bf16)
            rot = rotate(queries[:, base + NOPE : base + NOPE + ROPE].astype(f32), cosine, sine).astype(bf16)
            at = slice(h * APP, (h + 1) * APP)
            q_v[:, at, 0:LAT] = lat.reshape(TR_G, APP, LAT)
            q_v[:, at, LAT:KVW] = rot.reshape(TR_G, APP, ROPE)

    def start_softmax(t):
        count = app_ref[g * TR_G + t]
        fr = fresh[t * APP : (t + 1) * APP, :]
        s_refs[0][:, 0:APP] = lax.dot_general(q_v[t], fr, NT, preferred_element_type=f32)
        col = lax.broadcasted_iota(jnp.int32, (CHUNK, APP), 1)
        row = lax.rem(lax.broadcasted_iota(jnp.int32, (CHUNK, APP), 0), APP)
        allowed = (col <= row) & (col < count)
        for r in range(0, heads * APP, CHUNK):
            s = jnp.where(allowed, s_refs[0][r : r + CHUNK, 0:APP] * SCALE, NEG)
            top = jnp.max(s, axis=1, keepdims=True)
            p = jnp.exp2(s - top)
            m_ref[t, r : r + CHUNK, :] = jnp.broadcast_to(top, (CHUNK, 128))
            l_ref[t, r : r + CHUNK, :] = jnp.concatenate([p, jnp.zeros((CHUNK, 128 - APP), f32)], axis=1)
            p_ref[r : r + CHUNK, 0:APP] = p.astype(bf16)
        acc_ref[t] = jnp.dot(p_ref[:, 0:APP], fr[:, 0:LAT], preferred_element_type=f32)

    def scores(q, t, b):
        width = PHASES[q]
        for m in range(MAXP):
            source = pt_ref[m, g * TR_G + t] // G
            dz = rem(z - source // Y, Z)
            dy = rem(y - lax.rem(source, Y), Y)
            at = lax.rem(dz, 2) * (X * KC) + lax.rem(dy - dz + 2 * Z * Y, Y) * KC + dz // 2
            kts[b][m * width : (m + 1) * width, :] = pages[q][at]
        n = MAXP * width
        s_refs[b][:, 0:n] = lax.dot_general(q_v[t], kts[b][0:n, :], NT, preferred_element_type=f32)

    def combine(q, t, b):
        width = PHASES[q]
        n = MAXP * width
        col = lax.broadcasted_iota(jnp.int32, (1, n), 1)
        spot = col // width * PAGE + starts[q] + lax.rem(col, width)
        bias = jnp.where(spot < len_ref[g * TR_G + t], 0.0, NEG)
        for r in range(0, heads * APP, CHUNK):
            at = slice(r, r + CHUNK)
            s = s_refs[b][at, 0:n] * SCALE + bias
            old = m_ref[t, at, :]
            top = jnp.maximum(old, jnp.max(s, axis=1, keepdims=True))
            keep = jnp.exp2(old - top)
            m_ref[t, at, :] = top
            total = l_ref[t, at, :] * keep
            for j in range(0, n, 128):
                p = jnp.exp2(s[:, j : j + 128] - top)
                total = total + p
                p_ref[at, j : j + 128] = p.astype(bf16)
            l_ref[t, at, :] = total
            for j in range(0, LAT, 128):
                acc_ref[t, at, j : j + 128] = acc_ref[t, at, j : j + 128] * keep
        acc_ref[t] = acc_ref[t] + jnp.dot(p_ref[:, 0:n], kts[b][0:n, 0:LAT], preferred_element_type=f32)

    def finish(t):
        for r in range(0, heads * APP, CHUNK):
            total = jnp.sum(l_ref[t, r : r + CHUNK, :], axis=1, keepdims=True)
            o = (acc_ref[t, r : r + CHUNK, :] * (1.0 / total)).astype(bf16)
            o_ref[r // APP : (r + CHUNK) // APP, t * APP : (t + 1) * APP, :] = o.reshape(CHUNK // APP, APP, LAT)

    kv_one()
    tok = lax.broadcasted_iota(jnp.int32, (APP, 1), 0)
    pos = jnp.concatenate([tok + len_ref[g * TR_G + t] for t in range(TR_G)], axis=0)
    angles = tables(pos, ROPE)
    kv_two()
    loads[3].wait()
    loads[4].wait()
    q_heads(0, heads // 2, angles)
    step_own(0)
    kv_three()
    q_heads(heads // 2, heads, angles)
    step_own(1)
    kv_four()
    step_side(0)
    step_own(2)
    fr_s.wait()
    start_softmax(0)
    start_softmax(1)
    step_far(0)
    step_side(1)
    start_softmax(2)
    start_softmax(3)
    step_own(3)

    before = {
        (0, 0): [(step_done, 0)],
        (0, 2): [(step_far, 1), (step_side, 2)],
        (1, 0): [(step_done, 1)],
        (1, 1): [(step_far, 2)],
        (1, 2): [(step_side, 3)],
        (2, 0): [(step_done, 2)],
        (2, 2): [(step_far, 3)],
        (3, 0): [(step_done, 3)],
    }
    units = [(q, t) for q in range(n_ph) for t in range(TR_G)]
    for i, (q, t) in enumerate(units):
        for step, arg in before.get((q, t), ()):
            step(arg)
        scores(q, t, i % 2)
        if i > 0:
            pq, pt = units[i - 1]
            combine(pq, pt, (i - 1) % 2)
            if pq == n_ph - 1:
                finish(pt)
    combine(*units[-1], (len(units) - 1) % 2)
    finish(TR_G - 1)

    loads[5].wait()
    valid = jnp.concatenate([tok < app_ref[g * TR_G + t] for t in range(TR_G)], axis=0)
    outs = []
    for part in range(4):
        for h in range(part * heads // 4, (part + 1) * heads // 4):
            o = jnp.dot(o_ref[h], wuv[:, h * VHEAD : (h + 1) * VHEAD], preferred_element_type=f32)
            out_v[:, h * VHEAD : (h + 1) * VHEAD] = jnp.where(valid, o, 0.0).astype(bf16)
        wide = heads * VHEAD // 4
        at = pl.ds(part * wide, wide)
        copy = pltpu.make_async_copy(out_v.at[:, at], out_hbm.at[:, at], out_sem.at[part])
        copy.start()
        outs.append(copy)

    for q in range(n_ph):
        for k in range(KC):
            remote(k, lambda: first(q, k).wait_send())
        to_x(q, x, 0, dev_r).wait_send()
        to_x(q, x, 1, dev_l).wait_send()
        relay(q, xl, 0, dev_r).wait_send()
        relay(q, xr, 1, dev_l).wait_send()
        for n in range(4):
            to_sib(q, n).wait_send()
    for copy in outs:
        copy.wait()


def body(Z, Y, X, hidden, w_dkv, kv_gain, queries, w_uk, w_uv, store, page_table, cached_len, app_len):
    rows = hidden.shape[0]
    heads = w_uk.shape[1] // NOPE
    G = Z * Y
    KC = Z // 2
    n_ph = len(PHASES)
    any_spec = pl.BlockSpec(memory_space=pl.ANY)
    smem = pl.BlockSpec(memory_space=pltpu.SMEM)
    vmem = pl.BlockSpec(memory_space=pltpu.VMEM)
    hrows = rows // 2
    traj = heads * APP
    widest = MAXP * max(PHASES)
    VM, DMA = pltpu.VMEM, pltpu.SemaphoreType.DMA
    return pl.pallas_call(
        functools.partial(kernel, Z, Y, X),
        out_shape=jax.ShapeDtypeStruct((rows, heads * VHEAD), bf16),
        in_specs=[smem, smem, smem, vmem] + [any_spec] * 6,
        out_specs=any_spec,
        scratch_shapes=[
            VM(store.shape, bf16),
            VM(hidden.shape, bf16),
            VM((KVW, hidden.shape[1]), bf16),
            VM(queries.shape, bf16),
            VM(w_uk.shape, bf16),
            VM(w_uv.shape, bf16),
            VM((TR_G, traj, KVW), bf16),
            VM((rows, KVW), f32),
            VM((hrows, KVW), f32),
            VM((hrows, KVW), f32),
            VM((3, hrows // X, KVW), f32),
            VM((rows, KVW), bf16),
            VM((TR_G, traj, 128), f32),
            VM((TR_G, traj, 128), f32),
            VM((TR_G, traj, LAT), f32),
            VM((traj, widest), f32),
            VM((traj, widest), f32),
            VM((traj, widest), bf16),
            VM((widest, KVW), bf16),
            VM((widest, KVW), bf16),
            VM((heads, rows, LAT), bf16),
            VM((rows, heads * VHEAD), bf16),
            DMA((6,)),
            DMA((4,)),
            DMA((n_ph, KC)),
            DMA((n_ph, KC)),
            DMA((n_ph, 2)),
            DMA((n_ph, 2)),
            DMA((n_ph, 2)),
            DMA((n_ph, 2)),
            DMA((n_ph, 4)),
            DMA((n_ph, 4)),
            DMA((8,)),
            DMA((8,)),
        ]
        + [VM((KC, width, KVW), bf16) for width in PHASES]
        + [VM((G, width, KVW), bf16) for width in PHASES],
        compiler_params=pltpu.CompilerParams(
            collective_id=0, has_side_effects=True, vmem_limit_bytes=60 * 1024 * 1024
        ),
        name="resume",
    )(page_table.T, cached_len, app_len, kv_gain[None, :], hidden, w_dkv.T, queries, w_uk, w_uv, store)


def solution(mesh):
    X = mesh.shape["tp"] // 2
    Y = X
    Z = mesh.shape["grp"] // Y
    in_specs = (
        P("grp", "tp"),
        P("tp", None),
        P(),
        P("grp", "tp"),
        P(None, "tp"),
        P(None, "tp"),
        P("grp", None, None),
        P(),
        P(),
        P(),
    )
    return jax.shard_map(
        functools.partial(body, Z, Y, X), mesh=mesh, in_specs=in_specs, out_specs=P("grp", "tp"), check_vma=False
    )
```

```python
import functools
import math

import jax
import jax.numpy as jnp
from jax import lax
from jax.experimental import pallas as pl
from jax.experimental.pallas import tpu as pltpu
from jax.sharding import PartitionSpec as P

MESH = pl.DeviceIdType.MESH
NOPE = 128
ROPE = 64
LAT = 512
VHEAD = 128
PAGE = 128
MAXP = 8
TR_G = 4
APP = 64
KVW = LAT + ROPE
NEG = -1e30
NT = (((1,), (1,)), ((), ()))
PHASES = (32, 32, 32, 32)
CHUNK = 128
GATHER = 3
DIRECT = (((0, 0), (0, 1), (0, 2), (1, 0)), ((0, 3), (7, 0), (1, 1), (7, 3)))
NDIR = len(DIRECT[0])
SIDE = NDIR + 4 * GATHER
SCALE = math.log2(math.e) / math.sqrt(NOPE + ROPE)
bf16, f32 = jnp.bfloat16, jnp.float32


def rem(a, n):
    return lax.rem(a + n, n)


def tables(pos, width):
    half = width // 2
    lane = lax.rem(lax.broadcasted_iota(jnp.int32, (1, width), 1), half)
    freq = jnp.exp(lane.astype(f32) * (-2.0 * math.log(10000.0) / width))
    angle = pos.astype(f32) * freq
    sign = jnp.where(lax.broadcasted_iota(jnp.int32, (1, width), 1) < half, -1.0, 1.0)
    return jnp.cos(angle), jnp.sin(angle) * sign


def rotate(vec, cosine, sine):
    half = vec.shape[1] // 2
    swapped = jnp.concatenate([vec[:, half:], vec[:, :half]], axis=1)
    return vec * cosine + swapped * sine


def kernel(
    Z, Y, X,
    pt_ref, len_ref, app_ref, gain_ref, hidden_hbm, wdkv_hbm, queries_hbm, wuk_hbm, wuv_hbm, store_hbm,
    out_v,
    *scratch,
):
    n_ph = len(PHASES)
    (store_v, hidden, wdkv, queries, wuk, wuv, q_v, kv_part, kv_half, kv_sib, kv_in, fresh,
     m_ref, l_ref, acc_ref, s_a, s_b, p_ref, kt_a, kt_b, o_ref,
     load_sem, send1, recv1, sendx, recvx, sendr, recvr, sends, recvs, kvsend, kvrecv) = scratch[: -2 * n_ph]
    stage = scratch[-2 * n_ph : -n_ph]
    pages = scratch[-n_ph:]
    s_refs, kts = (s_a, s_b), (kt_a, kt_b)
    G = Z * Y
    g = lax.axis_index("grp")
    tp = lax.axis_index("tp")
    z, y = g // Y, lax.rem(g, Y)
    x, c = tp // 2, lax.rem(tp, 2)
    heads = wuk.shape[1] // NOPE
    rows = hidden.shape[0]
    starts = [sum(PHASES[:i]) for i in range(n_ph)]

    loads = [
        pltpu.make_async_copy(src, dst, load_sem.at[i])
        for i, (src, dst) in enumerate(
            ((store_hbm, store_v), (hidden_hbm, hidden), (wdkv_hbm, wdkv), (queries_hbm, queries),
             (wuk_hbm, wuk), (wuv_hbm, wuv))
        )
    ]
    for i in (1, 2, 0):
        loads[i].start()

    xr, xl, xo = rem(x + 1, X), rem(x - 1, X), rem(x + 2, X)
    dev_r, dev_l, dev_o, dev_s = (
        (g, xr * 2 + c), (g, xl * 2 + c), (g, xo * 2 + c), (g, x * 2 + 1 - c)
    )

    def gathered(k):
        dz = jnp.where(c == 0, 2 + 2 * k, (3, 5, jnp.where(x < 2, 1, Z - 1))[k])
        dy = lax.rem(dz + x, Y)
        if k == 2:
            dy = jnp.where(c == 0, dy, jnp.where(x < 2, 2 + x, x - 1))
        return dz, dy

    def direct(j):
        zero, one = DIRECT[0][j], DIRECT[1][j]
        return jnp.where(c == 0, zero[0], one[0]), jnp.where(c == 0, zero[1], one[1])

    def remote(j, fn):
        if j == GATHER:
            pl.when(c == 1)(fn)
        else:
            fn()

    moves = [gathered(k) for k in range(GATHER)] + [direct(j) for j in range(len(DIRECT[0]))]

    def group(n, way):
        dz, dy = moves[n]
        return rem(z + way * dz, Z) * Y + rem(y + way * dy, Y)

    barrier = pltpu.get_barrier_semaphore()

    def greet(dev):
        pl.semaphore_signal(barrier, inc=1, device_id=dev, device_id_type=MESH)

    for dev in (dev_r, dev_l, dev_o, dev_s):
        greet(dev)
    for n in range(len(moves)):
        remote(n, lambda: greet((group(n, -1), tp)))

    def slot_of(t, m):
        source = pt_ref[m, g * TR_G + t] // G
        dz = rem(z - source // Y, Z)
        dy = rem(y - lax.rem(source, Y), Y)
        who = lax.rem(dy - dz + Z, Y)
        gather = jnp.where(lax.rem(dz, 2) == 0, NDIR, SIDE + NDIR) + who * GATHER + dz // 2 - 1
        same = jnp.where(dy == 3, SIDE, dy)
        after = jnp.where(dy == 0, 3, jnp.where(dy == 1, SIDE + 2, SIDE + NDIR + (dy - 2) * GATHER + 2))
        ahead = jnp.where(dy == 0, SIDE + 1, jnp.where(dy == 3, SIDE + 3, SIDE + NDIR + (dy + 1) * GATHER + 2))
        return jnp.where(dz == 0, same, jnp.where(dz == 1, after, jnp.where(dz == Z - 1, ahead, gather)))

    places = [[slot_of(t, m) for m in range(MAXP)] for t in range(TR_G)]

    def find(dest):
        found = jnp.int32(0)
        for t in range(TR_G):
            for m in range(MAXP):
                value = pt_ref[m, dest * TR_G + t]
                found = found + jnp.where(value // G == g, lax.rem(value, G), 0)
        return found

    picks = [find(group(n, 1)) for n in range(len(moves))]

    def rcopy(src, dst, ss, rs, dev):
        return pltpu.make_async_remote_copy(
            src_ref=src, dst_ref=dst, send_sem=ss, recv_sem=rs, device_id=dev, device_id_type=MESH
        )

    def some(q, ref, first_slot, count):
        return ref.at[pl.ds(2 * first_slot, 2 * count)]

    def mine(who):
        return c * SIDE + NDIR + who * GATHER

    def first(q, n):
        at = mine(x) + n if n < GATHER else c * SIDE + n - GATHER
        return rcopy(
            some(q, stage[q], n, 1), some(q, pages[q], at, 1), send1.at[q, n], recv1.at[q, n], (group(n, 1), tp)
        )

    def prepare(n):
        page = store_v[picks[n]]
        lat, rope = page[0:LAT, :].T, page[LAT:KVW, :].T
        for q in range(n_ph):
            for e in range(2):
                unit = PHASES[q] // 2
                part = slice(starts[q] + e * unit, starts[q] + (e + 1) * unit)
                stage[q][2 * n + e, :, 0:LAT] = lat[part, :]
                stage[q][2 * n + e, :, LAT:KVW] = rope[part, :]

    hrows = rows // 2
    brows = hrows // X
    row0 = c * hrows + x * brows

    sib_kv = rcopy(kv_part.at[pl.ds((1 - c) * hrows, hrows)], kv_sib, kvsend.at[0], kvrecv.at[0], dev_s)
    kv_x = [
        rcopy(kv_half.at[pl.ds(xx * brows, brows)], kv_in.at[n], kvsend.at[1 + n], kvrecv.at[1 + n], dev)
        for n, (xx, dev) in enumerate(((xr, dev_r), (xl, dev_l), (xo, dev_o)))
    ]
    block = fresh.at[pl.ds(row0, brows)]
    fr_x = [
        rcopy(block, block, kvsend.at[4 + n], kvrecv.at[4 + n], dev)
        for n, dev in enumerate((dev_r, dev_l, dev_o))
    ]
    half = fresh.at[pl.ds(c * hrows, hrows)]
    fr_s = rcopy(half, half, kvsend.at[7], kvrecv.at[7], dev_s)

    def kv_two():
        sib_kv.wait()
        kv_half[...] = kv_part[pl.ds(c * hrows, hrows), :] + kv_sib[...]
        for copy in kv_x:
            copy.start()

    def kv_three():
        for copy in kv_x:
            copy.wait()
        kv = kv_half[pl.ds(x * brows, brows), :] + kv_in[0] + kv_in[1] + kv_in[2]
        lat = kv[:, :LAT]
        factor = lax.rsqrt(jnp.mean(lat * lat, axis=-1, keepdims=True) + 1e-06)
        lat = lat * factor * gain_ref[...]
        mypos = len_ref[g * TR_G + row0 // APP] + lax.rem(row0, APP)
        mycos, mysin = tables(mypos + lax.broadcasted_iota(jnp.int32, (brows, 1), 0), ROPE)
        fresh[pl.ds(row0, brows), 0:LAT] = lat.astype(bf16)
        fresh[pl.ds(row0, brows), LAT:KVW] = rotate(kv[:, LAT:], mycos, mysin).astype(bf16)
        for copy in fr_x:
            copy.start()

    def kv_four():
        for copy in fr_x:
            copy.wait()
        fr_s.start()

    loads[1].wait()
    loads[2].wait()
    kv_part[...] = lax.dot_general(hidden[...], wdkv[...], NT, preferred_element_type=f32)
    loads[0].wait()
    for load in loads[3:]:
        load.start()
    for n in range(GATHER):
        prepare(n)
    pl.semaphore_wait(barrier, len(moves) + 3 + c)
    sib_kv.start()
    for n in range(GATHER):
        first(0, n).start()
    kv_two()
    for n in range(GATHER, len(moves)):
        prepare(n)
    for q in range(1, n_ph + 1):
        if q < n_ph:
            for n in range(GATHER):
                first(q, n).start()
        for n in range(GATHER, len(moves)):
            remote(n, lambda: first(q - 1, n).start())

    @pl.when(c == 0)
    def _():
        for q in range(n_ph):
            for e in range(2):
                pages[q][e] = stage[q][2 * GATHER + e]

    def to_x(q, who, n, dev):
        part = some(q, pages[q], mine(who), GATHER)
        return rcopy(part, part, sendx.at[q, n], recvx.at[q, n], dev)

    def relay(q, who, n, dev):
        part = pages[q].at[pl.ds(2 * mine(who) + n * GATHER, GATHER)]
        return rcopy(part, part, sendr.at[q, n], recvr.at[q, n], dev)

    def shared(q, n, cls):
        if n == 4:
            return some(q, pages[q], cls * SIDE, NDIR)
        return some(q, pages[q], cls * SIDE + NDIR + (x, xl, xr, xo)[n] * GATHER, GATHER)

    def to_sib(q, n):
        part = shared(q, n, c)
        return rcopy(part, part, sends.at[q, n], recvs.at[q, n], dev_s)

    def from_sib(q, n):
        part = shared(q, n, 1 - c)
        return rcopy(part, part, sends.at[q, n], recvs.at[q, n], dev_s)

    def step_own(q):
        for n in range(GATHER):
            first(q, n).wait_recv()
        to_x(q, x, 0, dev_r).start()
        to_x(q, x, 1, dev_l).start()
        to_sib(q, 0).start()

    def step_direct(q):
        for n in range(GATHER, len(moves)):
            remote(n, lambda: first(q, n).wait_recv())
        to_sib(q, 4).start()

    def step_side(q):
        to_x(q, xl, 0, dev_r).wait_recv()
        relay(q, xl, 0, dev_r).start()
        to_sib(q, 1).start()
        to_x(q, xr, 1, dev_l).wait_recv()
        relay(q, xr, 1, dev_l).start()
        to_sib(q, 2).start()

    def step_far(q):
        relay(q, xo, 0, dev_r).wait_recv()
        relay(q, xo, 1, dev_l).wait_recv()
        to_sib(q, 3).start()

    def step_done(q):
        step_direct(q)
        for n in range(5):
            from_sib(q, n).wait_recv()

    def q_heads(first_head, last_head, angles):
        cosine, sine = angles
        for h in range(first_head, last_head):
            base = h * (NOPE + ROPE)
            lat = lax.dot_general(
                queries[:, base : base + NOPE], wuk[:, h * NOPE : (h + 1) * NOPE], NT, preferred_element_type=f32
            ).astype(bf16)
            rot = rotate(queries[:, base + NOPE : base + NOPE + ROPE].astype(f32), cosine, sine).astype(bf16)
            at = slice(h * APP, (h + 1) * APP)
            q_v[:, at, 0:LAT] = lat.reshape(TR_G, APP, LAT)
            q_v[:, at, LAT:KVW] = rot.reshape(TR_G, APP, ROPE)

    def start_softmax(t):
        count = app_ref[g * TR_G + t]
        fr = fresh[t * APP : (t + 1) * APP, :]
        s_refs[0][:, 0:APP] = lax.dot_general(q_v[t], fr, NT, preferred_element_type=f32)
        col = lax.broadcasted_iota(jnp.int32, (CHUNK, APP), 1)
        row = lax.rem(lax.broadcasted_iota(jnp.int32, (CHUNK, APP), 0), APP)
        allowed = (col <= row) & (col < count)
        for r in range(0, heads * APP, CHUNK):
            s = jnp.where(allowed, s_refs[0][r : r + CHUNK, 0:APP] * SCALE, NEG)
            top = jnp.max(s, axis=1, keepdims=True)
            p = jnp.exp2(s - top)
            m_ref[t, r : r + CHUNK, :] = jnp.broadcast_to(top, (CHUNK, 128))
            l_ref[t, r : r + CHUNK, :] = jnp.concatenate([p, jnp.zeros((CHUNK, 128 - APP), f32)], axis=1)
            p_ref[r : r + CHUNK, 0:APP] = p.astype(bf16)
        acc_ref[t] = jnp.dot(p_ref[:, 0:APP], fr[:, 0:LAT], preferred_element_type=f32)

    def scores(q, t, b):
        width = PHASES[q]
        for m in range(MAXP):
            for e in range(2):
                at = m * width + e * (width // 2)
                kts[b][at : at + width // 2, :] = pages[q][2 * places[t][m] + e]
        n = MAXP * width
        s_refs[b][:, 0:n] = lax.dot_general(q_v[t], kts[b][0:n, :], NT, preferred_element_type=f32)

    def combine(q, t, b):
        width = PHASES[q]
        n = MAXP * width
        col = lax.broadcasted_iota(jnp.int32, (1, n), 1)
        spot = col // width * PAGE + starts[q] + lax.rem(col, width)
        bias = jnp.where(spot < len_ref[g * TR_G + t], 0.0, NEG)
        for r in range(0, heads * APP, CHUNK):
            at = slice(r, r + CHUNK)
            s = s_refs[b][at, 0:n] * SCALE + bias
            old = m_ref[t, at, :]
            top = jnp.maximum(old, jnp.max(s, axis=1, keepdims=True))
            keep = jnp.exp2(old - top)
            m_ref[t, at, :] = top
            total = l_ref[t, at, :] * keep
            for j in range(0, n, 128):
                p = jnp.exp2(s[:, j : j + 128] - top)
                total = total + p
                p_ref[at, j : j + 128] = p.astype(bf16)
            l_ref[t, at, :] = total
            for j in range(0, LAT, 128):
                acc_ref[t, at, j : j + 128] = acc_ref[t, at, j : j + 128] * keep
        acc_ref[t] = acc_ref[t] + jnp.dot(p_ref[:, 0:n], kts[b][0:n, 0:LAT], preferred_element_type=f32)

    def finish(t):
        for r in range(0, heads * APP, CHUNK):
            total = jnp.sum(l_ref[t, r : r + CHUNK, :], axis=1, keepdims=True)
            o = (acc_ref[t, r : r + CHUNK, :] * (1.0 / total)).astype(bf16)
            o_ref[r // APP : (r + CHUNK) // APP, t * APP : (t + 1) * APP, :] = o.reshape(CHUNK // APP, APP, LAT)

    tok = lax.broadcasted_iota(jnp.int32, (APP, 1), 0)
    pos = jnp.concatenate([tok + len_ref[g * TR_G + t] for t in range(TR_G)], axis=0)
    angles = tables(pos, ROPE)
    loads[3].wait()
    loads[4].wait()
    q_heads(0, heads // 2, angles)
    kv_three()
    q_heads(heads // 2, heads, angles)
    step_own(0)
    kv_four()
    step_own(1)
    step_side(0)
    fr_s.wait()
    start_softmax(0)
    step_own(2)
    start_softmax(1)
    step_far(0)
    step_side(1)
    start_softmax(2)
    start_softmax(3)

    before = {
        (0, 0): [(step_done, 0), (step_own, 3)],
        (0, 2): [(step_far, 1), (step_side, 2)],
        (1, 0): [(step_done, 1)],
        (1, 2): [(step_far, 2), (step_side, 3)],
        (2, 0): [(step_done, 2)],
        (2, 2): [(step_far, 3)],
        (3, 0): [(step_done, 3)],
    }
    units = [(q, t) for q in range(n_ph) for t in range(TR_G)]
    for i, (q, t) in enumerate(units):
        steps = before.get((q, t), ())
        if i > 0 and steps:
            combine(*units[i - 1], (i - 1) % 2)
        for step, arg in steps:
            step(arg)
        scores(q, t, i % 2)
        if i > 0:
            pq, pt = units[i - 1]
            if not steps:
                combine(pq, pt, (i - 1) % 2)
            if pq == n_ph - 1:
                finish(pt)
    combine(*units[-1], (len(units) - 1) % 2)
    finish(TR_G - 1)

    loads[5].wait()
    valid = jnp.concatenate([tok < app_ref[g * TR_G + t] for t in range(TR_G)], axis=0)
    for part in range(4):
        for h in range(part * heads // 4, (part + 1) * heads // 4):
            o = jnp.dot(o_ref[h], wuv[:, h * VHEAD : (h + 1) * VHEAD], preferred_element_type=f32)
            out_v[:, h * VHEAD : (h + 1) * VHEAD] = jnp.where(valid, o, 0.0).astype(bf16)
    for q in range(n_ph):
        for n in range(len(moves)):
            remote(n, lambda: first(q, n).wait_send())
        to_x(q, x, 0, dev_r).wait_send()
        to_x(q, x, 1, dev_l).wait_send()
        relay(q, xl, 0, dev_r).wait_send()
        relay(q, xr, 1, dev_l).wait_send()
        for n in range(5):
            to_sib(q, n).wait_send()


def body(Z, Y, X, hidden, w_dkv, kv_gain, queries, w_uk, w_uv, store, page_table, cached_len, app_len):
    rows = hidden.shape[0]
    heads = w_uk.shape[1] // NOPE
    G = Z * Y
    n_ph = len(PHASES)
    any_spec = pl.BlockSpec(memory_space=pl.ANY)
    smem = pl.BlockSpec(memory_space=pltpu.SMEM)
    vmem = pl.BlockSpec(memory_space=pltpu.VMEM)
    hrows = rows // 2
    traj = heads * APP
    widest = MAXP * max(PHASES)
    VM, DMA = pltpu.VMEM, pltpu.SemaphoreType.DMA
    return pl.pallas_call(
        functools.partial(kernel, Z, Y, X),
        out_shape=pltpu.VMEM((rows, heads * VHEAD), bf16),
        in_specs=[smem, smem, smem, vmem] + [any_spec] * 6,
        out_specs=vmem,
        scratch_shapes=[
            VM(store.shape, bf16),
            VM(hidden.shape, bf16),
            VM((KVW, hidden.shape[1]), bf16),
            VM(queries.shape, bf16),
            VM(w_uk.shape, bf16),
            VM(w_uv.shape, bf16),
            VM((TR_G, traj, KVW), bf16),
            VM((rows, KVW), f32),
            VM((hrows, KVW), f32),
            VM((hrows, KVW), f32),
            VM((3, hrows // X, KVW), f32),
            VM((rows, KVW), bf16),
            VM((TR_G, traj, 128), f32),
            VM((TR_G, traj, 128), f32),
            VM((TR_G, traj, LAT), f32),
            VM((traj, widest), f32),
            VM((traj, widest), f32),
            VM((traj, widest), bf16),
            VM((widest, KVW), bf16),
            VM((widest, KVW), bf16),
            VM((heads, rows, LAT), bf16),
            DMA((6,)),
            DMA((n_ph, GATHER + NDIR)),
            DMA((n_ph, GATHER + NDIR)),
            DMA((n_ph, 2)),
            DMA((n_ph, 2)),
            DMA((n_ph, 2)),
            DMA((n_ph, 2)),
            DMA((n_ph, 5)),
            DMA((n_ph, 5)),
            DMA((8,)),
            DMA((8,)),
        ]
        + [VM((2 * (GATHER + NDIR), width // 2, KVW), bf16) for width in PHASES]
        + [VM((2 * G, width // 2, KVW), bf16) for width in PHASES],
        compiler_params=pltpu.CompilerParams(
            collective_id=0, has_side_effects=True, vmem_limit_bytes=60 * 1024 * 1024
        ),
        name="resume",
    )(page_table.T, cached_len, app_len, kv_gain[None, :], hidden, w_dkv.T, queries, w_uk, w_uv, store)


def solution(mesh):
    X = mesh.shape["tp"] // 2
    Y = X
    Z = mesh.shape["grp"] // Y
    in_specs = (
        P("grp", "tp"),
        P("tp", None),
        P(),
        P("grp", "tp"),
        P(None, "tp"),
        P(None, "tp"),
        P("grp", None, None),
        P(),
        P(),
        P(),
    )
    return jax.shard_map(
        functools.partial(body, Z, Y, X), mesh=mesh, in_specs=in_specs, out_specs=P("grp", "tp"), check_vma=False
    )
```

```python
import functools
import math

import jax
import jax.numpy as jnp
from jax import lax
from jax.experimental import pallas as pl
from jax.experimental.pallas import tpu as pltpu
from jax.sharding import PartitionSpec as P

MESH = pl.DeviceIdType.MESH
NOPE = 128
ROPE = 64
LAT = 512
VHEAD = 128
PAGE = 128
MAXP = 8
TR_G = 4
APP = 64
KVW = LAT + ROPE
NEG = -1e30
NT = (((1,), (1,)), ((), ()))
PHASES = (32, 32, 32, 32)
CHUNK = 128
GATHER = 3
DIRECT = (((0, 0), (0, 1), (0, 2), (1, 0)), ((0, 3), (7, 0), (1, 1), (7, 3)))
NDIR = len(DIRECT[0])
SIDE = NDIR + 4 * GATHER
SCALE = math.log2(math.e) / math.sqrt(NOPE + ROPE)
bf16, f32 = jnp.bfloat16, jnp.float32


def rem(a, n):
    return lax.rem(a + n, n)


def tables(pos, width):
    half = width // 2
    lane = lax.rem(lax.broadcasted_iota(jnp.int32, (1, width), 1), half)
    freq = jnp.exp(lane.astype(f32) * (-2.0 * math.log(10000.0) / width))
    angle = pos.astype(f32) * freq
    sign = jnp.where(lax.broadcasted_iota(jnp.int32, (1, width), 1) < half, -1.0, 1.0)
    return jnp.cos(angle), jnp.sin(angle) * sign


def rotate(vec, cosine, sine):
    half = vec.shape[1] // 2
    swapped = jnp.concatenate([vec[:, half:], vec[:, :half]], axis=1)
    return vec * cosine + swapped * sine


def kernel(
    Z, Y, X,
    pt_ref, len_ref, app_ref, gain_ref, hidden_hbm, wdkv_hbm, queries_hbm, wuk_hbm, wuv_hbm, store_hbm,
    out_v,
    *scratch,
):
    n_ph = len(PHASES)
    (store_v, hidden, wdkv, queries, wuk, wuv, q_v, kv_part, kv_half, kv_sib, kv_in, fresh,
     m_ref, l_ref, acc_ref, s_a, s_b, p_ref, kt_a, kt_b, o_ref,
     load_sem, send1, recv1, sendx, recvx, sendr, recvr, sends, recvs, kvsend, kvrecv) = scratch[: -2 * n_ph]
    stage = scratch[-2 * n_ph : -n_ph]
    pages = scratch[-n_ph:]
    s_refs, kts = (s_a, s_b), (kt_a, kt_b)
    G = Z * Y
    g = lax.axis_index("grp")
    tp = lax.axis_index("tp")
    z, y = g // Y, lax.rem(g, Y)
    x, c = tp // 2, lax.rem(tp, 2)
    heads = wuk.shape[1] // NOPE
    rows = hidden.shape[0]
    starts = [sum(PHASES[:i]) for i in range(n_ph)]

    loads = [
        pltpu.make_async_copy(src, dst, load_sem.at[i])
        for i, (src, dst) in enumerate(
            ((store_hbm, store_v), (hidden_hbm, hidden), (wdkv_hbm, wdkv), (queries_hbm, queries),
             (wuk_hbm, wuk), (wuv_hbm, wuv))
        )
    ]
    for i in (1, 2, 0):
        loads[i].start()

    xr, xl, xo = rem(x + 1, X), rem(x - 1, X), rem(x + 2, X)
    dev_r, dev_l, dev_o, dev_s = (
        (g, xr * 2 + c), (g, xl * 2 + c), (g, xo * 2 + c), (g, x * 2 + 1 - c)
    )

    def gathered(k):
        dz = jnp.where(c == 0, 2 + 2 * k, (3, 5, jnp.where(x < 2, 1, Z - 1))[k])
        dy = lax.rem(dz + x, Y)
        if k == 2:
            dy = jnp.where(c == 0, dy, jnp.where(x < 2, 2 + x, x - 1))
        return dz, dy

    def direct(j):
        zero, one = DIRECT[0][j], DIRECT[1][j]
        return jnp.where(c == 0, zero[0], one[0]), jnp.where(c == 0, zero[1], one[1])

    def remote(j, fn):
        if j == GATHER:
            pl.when(c == 1)(fn)
        else:
            fn()

    moves = [gathered(k) for k in range(GATHER)] + [direct(j) for j in range(len(DIRECT[0]))]

    def group(n, way):
        dz, dy = moves[n]
        return rem(z + way * dz, Z) * Y + rem(y + way * dy, Y)

    barrier = pltpu.get_barrier_semaphore()

    def greet(dev):
        pl.semaphore_signal(barrier, inc=1, device_id=dev, device_id_type=MESH)

    for dev in (dev_r, dev_l, dev_o, dev_s):
        greet(dev)
    for n in range(len(moves)):
        remote(n, lambda: greet((group(n, -1), tp)))

    def slot_of(t, m):
        source = pt_ref[m, g * TR_G + t] // G
        dz = rem(z - source // Y, Z)
        dy = rem(y - lax.rem(source, Y), Y)
        who = lax.rem(dy - dz + Z, Y)
        gather = jnp.where(lax.rem(dz, 2) == 0, NDIR, SIDE + NDIR) + who * GATHER + dz // 2 - 1
        same = jnp.where(dy == 3, SIDE, dy)
        after = jnp.where(dy == 0, 3, jnp.where(dy == 1, SIDE + 2, SIDE + NDIR + (dy - 2) * GATHER + 2))
        ahead = jnp.where(dy == 0, SIDE + 1, jnp.where(dy == 3, SIDE + 3, SIDE + NDIR + (dy + 1) * GATHER + 2))
        return jnp.where(dz == 0, same, jnp.where(dz == 1, after, jnp.where(dz == Z - 1, ahead, gather)))

    places = [[slot_of(t, m) for m in range(MAXP)] for t in range(TR_G)]

    def find(dest):
        found = jnp.int32(0)
        for t in range(TR_G):
            for m in range(MAXP):
                value = pt_ref[m, dest * TR_G + t]
                found = found + jnp.where(value // G == g, lax.rem(value, G), 0)
        return found

    picks = [find(group(n, 1)) for n in range(len(moves))]

    def rcopy(src, dst, ss, rs, dev):
        return pltpu.make_async_remote_copy(
            src_ref=src, dst_ref=dst, send_sem=ss, recv_sem=rs, device_id=dev, device_id_type=MESH
        )

    def some(q, ref, first_slot, count):
        return ref.at[pl.ds(2 * first_slot, 2 * count)]

    def mine(who):
        return c * SIDE + NDIR + who * GATHER

    def first(q, n):
        at = mine(x) + n if n < GATHER else c * SIDE + n - GATHER
        return rcopy(
            some(q, stage[q], n, 1), some(q, pages[q], at, 1), send1.at[q, n], recv1.at[q, n], (group(n, 1), tp)
        )

    def prepare(n):
        page = store_v[picks[n]]
        lat, rope = page[0:LAT, :].T, page[LAT:KVW, :].T
        for q in range(n_ph):
            for e in range(2):
                unit = PHASES[q] // 2
                part = slice(starts[q] + e * unit, starts[q] + (e + 1) * unit)
                stage[q][2 * n + e, :, 0:LAT] = lat[part, :]
                stage[q][2 * n + e, :, LAT:KVW] = rope[part, :]

    hrows = rows // 2
    brows = hrows // X
    row0 = c * hrows + x * brows

    sib_kv = rcopy(kv_part.at[pl.ds((1 - c) * hrows, hrows)], kv_sib, kvsend.at[0], kvrecv.at[0], dev_s)
    kv_x = [
        rcopy(kv_half.at[pl.ds(xx * brows, brows)], kv_in.at[n], kvsend.at[1 + n], kvrecv.at[1 + n], dev)
        for n, (xx, dev) in enumerate(((xr, dev_r), (xl, dev_l), (xo, dev_o)))
    ]
    block = fresh.at[pl.ds(row0, brows)]
    fr_x = [
        rcopy(block, block, kvsend.at[4 + n], kvrecv.at[4 + n], dev)
        for n, dev in enumerate((dev_r, dev_l, dev_o))
    ]
    half = fresh.at[pl.ds(c * hrows, hrows)]
    fr_s = rcopy(half, half, kvsend.at[7], kvrecv.at[7], dev_s)

    def kv_two():
        sib_kv.wait()
        kv_half[...] = kv_part[pl.ds(c * hrows, hrows), :] + kv_sib[...]
        for copy in kv_x:
            copy.start()

    def kv_three():
        for copy in kv_x:
            copy.wait()
        kv = kv_half[pl.ds(x * brows, brows), :] + kv_in[0] + kv_in[1] + kv_in[2]
        lat = kv[:, :LAT]
        factor = lax.rsqrt(jnp.mean(lat * lat, axis=-1, keepdims=True) + 1e-06)
        lat = lat * factor * gain_ref[...]
        mypos = len_ref[g * TR_G + row0 // APP] + lax.rem(row0, APP)
        mycos, mysin = tables(mypos + lax.broadcasted_iota(jnp.int32, (brows, 1), 0), ROPE)
        fresh[pl.ds(row0, brows), 0:LAT] = lat.astype(bf16)
        fresh[pl.ds(row0, brows), LAT:KVW] = rotate(kv[:, LAT:], mycos, mysin).astype(bf16)
        for copy in fr_x:
            copy.start()

    def kv_four():
        for copy in fr_x:
            copy.wait()
        fr_s.start()

    loads[1].wait()
    loads[2].wait()
    kv_part[...] = lax.dot_general(hidden[...], wdkv[...], NT, preferred_element_type=f32)
    loads[0].wait()
    for load in loads[3:]:
        load.start()
    for n in range(GATHER):
        prepare(n)
    pl.semaphore_wait(barrier, len(moves) + 3 + c)
    sib_kv.start()
    for n in range(GATHER):
        first(0, n).start()
    kv_two()
    for n in range(GATHER, len(moves)):
        prepare(n)
    for q in range(1, n_ph + 1):
        if q < n_ph:
            for n in range(GATHER):
                first(q, n).start()
        for n in range(GATHER, len(moves)):
            remote(n, lambda: first(q - 1, n).start())

    @pl.when(c == 0)
    def _():
        for q in range(n_ph):
            for e in range(2):
                pages[q][e] = stage[q][2 * GATHER + e]

    def to_x(q, who, n, dev):
        part = some(q, pages[q], mine(who), GATHER)
        return rcopy(part, part, sendx.at[q, n], recvx.at[q, n], dev)

    def relay(q, who, n, dev):
        part = pages[q].at[pl.ds(2 * mine(who) + n * GATHER, GATHER)]
        return rcopy(part, part, sendr.at[q, n], recvr.at[q, n], dev)

    def shared(q, n, cls):
        if n == 4:
            return some(q, pages[q], cls * SIDE, NDIR)
        return some(q, pages[q], cls * SIDE + NDIR + (x, xl, xr, xo)[n] * GATHER, GATHER)

    def to_sib(q, n):
        part = shared(q, n, c)
        return rcopy(part, part, sends.at[q, n], recvs.at[q, n], dev_s)

    def from_sib(q, n):
        part = shared(q, n, 1 - c)
        return rcopy(part, part, sends.at[q, n], recvs.at[q, n], dev_s)

    def step_own(q):
        for n in range(GATHER):
            first(q, n).wait_recv()
        to_x(q, x, 0, dev_r).start()
        to_x(q, x, 1, dev_l).start()
        to_sib(q, 0).start()

    def step_direct(q):
        for n in range(GATHER, len(moves)):
            remote(n, lambda: first(q, n).wait_recv())
        to_sib(q, 4).start()

    def step_side(q):
        to_x(q, xl, 0, dev_r).wait_recv()
        relay(q, xl, 0, dev_r).start()
        to_sib(q, 1).start()
        to_x(q, xr, 1, dev_l).wait_recv()
        relay(q, xr, 1, dev_l).start()
        to_sib(q, 2).start()

    def step_far(q):
        relay(q, xo, 0, dev_r).wait_recv()
        relay(q, xo, 1, dev_l).wait_recv()
        to_sib(q, 3).start()

    def step_done(q):
        step_direct(q)
        for n in range(5):
            from_sib(q, n).wait_recv()

    def q_heads(first_head, last_head, angles):
        cosine, sine = angles
        for h in range(first_head, last_head):
            base = h * (NOPE + ROPE)
            lat = lax.dot_general(
                queries[:, base : base + NOPE], wuk[:, h * NOPE : (h + 1) * NOPE], NT, preferred_element_type=f32
            ).astype(bf16)
            rot = rotate(queries[:, base + NOPE : base + NOPE + ROPE].astype(f32), cosine, sine).astype(bf16)
            at = slice(h * APP, (h + 1) * APP)
            q_v[:, at, 0:LAT] = lat.reshape(TR_G, APP, LAT)
            q_v[:, at, LAT:KVW] = rot.reshape(TR_G, APP, ROPE)

    def start_softmax(t):
        count = app_ref[g * TR_G + t]
        fr = fresh[t * APP : (t + 1) * APP, :]
        s_refs[0][:, 0:APP] = lax.dot_general(q_v[t], fr, NT, preferred_element_type=f32)
        col = lax.broadcasted_iota(jnp.int32, (CHUNK, APP), 1)
        row = lax.rem(lax.broadcasted_iota(jnp.int32, (CHUNK, APP), 0), APP)
        allowed = (col <= row) & (col < count)
        for r in range(0, heads * APP, CHUNK):
            s = jnp.where(allowed, s_refs[0][r : r + CHUNK, 0:APP] * SCALE, NEG)
            top = jnp.max(s, axis=1, keepdims=True)
            p = jnp.exp2(s - top)
            m_ref[t, r : r + CHUNK, :] = jnp.broadcast_to(top, (CHUNK, 128))
            l_ref[t, r : r + CHUNK, :] = jnp.concatenate([p, jnp.zeros((CHUNK, 128 - APP), f32)], axis=1)
            p_ref[r : r + CHUNK, 0:APP] = p.astype(bf16)
        acc_ref[t] = jnp.dot(p_ref[:, 0:APP], fr[:, 0:LAT], preferred_element_type=f32)

    def scores(q, t, b):
        width = PHASES[q]
        for m in range(MAXP):
            for e in range(2):
                at = m * width + e * (width // 2)
                kts[b][at : at + width // 2, :] = pages[q][2 * places[t][m] + e]
        n = MAXP * width
        s_refs[b][:, 0:n] = lax.dot_general(q_v[t], kts[b][0:n, :], NT, preferred_element_type=f32)

    def combine(q, t, b):
        width = PHASES[q]
        n = MAXP * width
        col = lax.broadcasted_iota(jnp.int32, (1, n), 1)
        spot = col // width * PAGE + starts[q] + lax.rem(col, width)
        bias = jnp.where(spot < len_ref[g * TR_G + t], 0.0, NEG)
        for r in range(0, heads * APP, CHUNK):
            at = slice(r, r + CHUNK)
            s = s_refs[b][at, 0:n] * SCALE + bias
            old = m_ref[t, at, :]
            top = jnp.maximum(old, jnp.max(s, axis=1, keepdims=True))
            keep = jnp.exp2(old - top)
            m_ref[t, at, :] = top
            total = l_ref[t, at, :] * keep
            for j in range(0, n, 128):
                p = jnp.exp2(s[:, j : j + 128] - top)
                total = total + p
                p_ref[at, j : j + 128] = p.astype(bf16)
            l_ref[t, at, :] = total
            for j in range(0, LAT, 128):
                acc_ref[t, at, j : j + 128] = acc_ref[t, at, j : j + 128] * keep
        acc_ref[t] = acc_ref[t] + jnp.dot(p_ref[:, 0:n], kts[b][0:n, 0:LAT], preferred_element_type=f32)

    def finish(t):
        for r in range(0, heads * APP, CHUNK):
            total = jnp.sum(l_ref[t, r : r + CHUNK, :], axis=1, keepdims=True)
            o = (acc_ref[t, r : r + CHUNK, :] * (1.0 / total)).astype(bf16)
            o_ref[r // APP : (r + CHUNK) // APP, t * APP : (t + 1) * APP, :] = o.reshape(CHUNK // APP, APP, LAT)

    tok = lax.broadcasted_iota(jnp.int32, (APP, 1), 0)
    pos = jnp.concatenate([tok + len_ref[g * TR_G + t] for t in range(TR_G)], axis=0)
    angles = tables(pos, ROPE)
    loads[3].wait()
    loads[4].wait()
    q_heads(0, heads // 2, angles)
    kv_three()
    q_heads(heads // 2, heads, angles)
    step_own(0)
    kv_four()
    step_own(1)
    step_side(0)
    fr_s.wait()
    start_softmax(0)
    step_own(2)
    start_softmax(1)
    step_far(0)
    step_side(1)
    start_softmax(2)
    start_softmax(3)

    before = {
        (0, 0): [(step_done, 0), (step_own, 3)],
        (0, 1): [(step_far, 1), (step_side, 2)],
        (1, 0): [(step_done, 1)],
        (1, 1): [(step_far, 2), (step_side, 3)],
        (2, 0): [(step_done, 2)],
        (2, 1): [(step_far, 3)],
        (3, 0): [(step_done, 3)],
    }
    units = [(q, t) for q in range(n_ph) for t in range(TR_G)]
    for i, (q, t) in enumerate(units):
        steps = before.get((q, t), ())
        if i > 0 and steps:
            combine(*units[i - 1], (i - 1) % 2)
        for step, arg in steps:
            step(arg)
        scores(q, t, i % 2)
        if i > 0:
            pq, pt = units[i - 1]
            if not steps:
                combine(pq, pt, (i - 1) % 2)
            if pq == n_ph - 1:
                finish(pt)
    combine(*units[-1], (len(units) - 1) % 2)
    finish(TR_G - 1)

    loads[5].wait()
    valid = jnp.concatenate([tok < app_ref[g * TR_G + t] for t in range(TR_G)], axis=0)
    for part in range(4):
        for h in range(part * heads // 4, (part + 1) * heads // 4):
            o = jnp.dot(o_ref[h], wuv[:, h * VHEAD : (h + 1) * VHEAD], preferred_element_type=f32)
            out_v[:, h * VHEAD : (h + 1) * VHEAD] = jnp.where(valid, o, 0.0).astype(bf16)
    for q in range(n_ph):
        for n in range(len(moves)):
            remote(n, lambda: first(q, n).wait_send())
        to_x(q, x, 0, dev_r).wait_send()
        to_x(q, x, 1, dev_l).wait_send()
        relay(q, xl, 0, dev_r).wait_send()
        relay(q, xr, 1, dev_l).wait_send()
        for n in range(5):
            to_sib(q, n).wait_send()


def body(Z, Y, X, hidden, w_dkv, kv_gain, queries, w_uk, w_uv, store, page_table, cached_len, app_len):
    rows = hidden.shape[0]
    heads = w_uk.shape[1] // NOPE
    G = Z * Y
    n_ph = len(PHASES)
    any_spec = pl.BlockSpec(memory_space=pl.ANY)
    smem = pl.BlockSpec(memory_space=pltpu.SMEM)
    vmem = pl.BlockSpec(memory_space=pltpu.VMEM)
    hrows = rows // 2
    traj = heads * APP
    widest = MAXP * max(PHASES)
    VM, DMA = pltpu.VMEM, pltpu.SemaphoreType.DMA
    return pl.pallas_call(
        functools.partial(kernel, Z, Y, X),
        out_shape=pltpu.VMEM((rows, heads * VHEAD), bf16),
        in_specs=[smem, smem, smem, vmem] + [any_spec] * 6,
        out_specs=vmem,
        scratch_shapes=[
            VM(store.shape, bf16),
            VM(hidden.shape, bf16),
            VM((KVW, hidden.shape[1]), bf16),
            VM(queries.shape, bf16),
            VM(w_uk.shape, bf16),
            VM(w_uv.shape, bf16),
            VM((TR_G, traj, KVW), bf16),
            VM((rows, KVW), f32),
            VM((hrows, KVW), f32),
            VM((hrows, KVW), f32),
            VM((3, hrows // X, KVW), f32),
            VM((rows, KVW), bf16),
            VM((TR_G, traj, 128), f32),
            VM((TR_G, traj, 128), f32),
            VM((TR_G, traj, LAT), f32),
            VM((traj, widest), f32),
            VM((traj, widest), f32),
            VM((traj, widest), bf16),
            VM((widest, KVW), bf16),
            VM((widest, KVW), bf16),
            VM((heads, rows, LAT), bf16),
            DMA((6,)),
            DMA((n_ph, GATHER + NDIR)),
            DMA((n_ph, GATHER + NDIR)),
            DMA((n_ph, 2)),
            DMA((n_ph, 2)),
            DMA((n_ph, 2)),
            DMA((n_ph, 2)),
            DMA((n_ph, 5)),
            DMA((n_ph, 5)),
            DMA((8,)),
            DMA((8,)),
        ]
        + [VM((2 * (GATHER + NDIR), width // 2, KVW), bf16) for width in PHASES]
        + [VM((2 * G, width // 2, KVW), bf16) for width in PHASES],
        compiler_params=pltpu.CompilerParams(
            collective_id=0, has_side_effects=True, vmem_limit_bytes=60 * 1024 * 1024
        ),
        name="resume",
    )(page_table.T, cached_len, app_len, kv_gain[None, :], hidden, w_dkv.T, queries, w_uk, w_uv, store)


def solution(mesh):
    X = mesh.shape["tp"] // 2
    Y = X
    Z = mesh.shape["grp"] // Y
    in_specs = (
        P("grp", "tp"),
        P("tp", None),
        P(),
        P("grp", "tp"),
        P(None, "tp"),
        P(None, "tp"),
        P("grp", None, None),
        P(),
        P(),
        P(),
    )
    return jax.shard_map(
        functools.partial(body, Z, Y, X), mesh=mesh, in_specs=in_specs, out_specs=P("grp", "tp"), check_vma=False
    )
```
